256 devices in a mesh: group: 16 (over y_lo, z), expert: 16 (over x, y_hi, core).
Axes of the slice: x: 4, y: 4 (y_hi: 2, y_lo: 2; y = y_hi * 2 + y_lo), z: 8, core: 2. Of those that a mesh axis runs over, the one named last changes fastest.
Arguments:
- train_inputs: float32 [256, 16, 1024], P(('group', 'expert')), as said below
- inv_factor: float32 [256, 1024, 1024], P(('group', 'expert')), as said below
- weights: float32 [256, 1024, 512], P(('group', 'expert')), as said below
- candidates: float32 [16, 4096], replicated, as said below
- test_ids: int32 [1024], replicated, may hold values from 0 to 4095
- basis: bfloat16 [512, 262144], P(None, ('group', 'expert')), may hold values from -0.25 to 0.25
- climatology: float32 [262144], P(('group', 'expert')), may hold values from -3 to 3
Outputs:
- field: bfloat16 [1024, 262144], P(None, ('group', 'expert'))
The draws below stay inside these ranges and needn't reach their ends.
Inputs may be any that keep to these rules, and one draw needn't show every extreme that they name: inv_factor[e] is lower triangular with L L^T = K + 0.1 I inverted, where K[r, s] = exp(-0.5 |x_r - x_s|^2) over the columns of train_inputs[e]. `train_inputs`: entries of magnitude below 2. `candidates`: entries of magnitude below 2. `weights`: entries of magnitude at most 0.6 * sqrt(256).
All inputs are finite; a program needn't handle non-finite values.
Results may differ from the reference program's by a relative error of at most 0.0045.
Values may be sent and summed in bfloat16 or wider, within the bound.
A program may use at most 64 MiB of HBM per device.

```python
import math
import jax
import jax.numpy as jnp
from jax import lax

DIN = 16
RUNS = 1024
OUT = 512
TESTS = 1024
CANDS = 4096
CELL_DEV = 1024
EXPERTS = 256
CELLS = 262144


noise_var = 0.1


def shared_offset(key):
    return jax.random.uniform(jax.random.fold_in(key, 101), (DIN,), jnp.float32, -0.25, 0.25)


def draw_train_inputs(key, part):
    offset = shared_offset(key)
    half_width = math.sqrt(12.0 / DIN)
    spread = jax.random.uniform(jax.random.fold_in(key, 102), (EXPERTS, DIN, RUNS), jnp.float32, -half_width, half_width)
    return offset[None, :, None] + spread


def draw_inv_factor(key, part):
    train_points = draw_train_inputs(key, part)
    identity = jnp.eye(RUNS, dtype=jnp.float32)

    def factor_one(points):
        squares = jnp.sum(points * points, axis=0)
        inner = jnp.dot(points.T, points, precision=lax.Precision.HIGHEST)
        gram = jnp.exp(-0.5 * (squares[:, None] + squares[None, :] - 2.0 * inner))
        gram = 0.5 * (gram + gram.T) + noise_var * identity
        lower = jnp.linalg.cholesky(gram)
        return jax.scipy.linalg.solve_triangular(lower, identity, lower=True)
    return lax.map(factor_one, train_points)


def draw_weights(key, part):
    scale = 0.2 * math.sqrt(EXPERTS)
    values = jax.random.normal(jax.random.fold_in(key, 106), (EXPERTS, RUNS, OUT), jnp.float32)
    return jnp.clip(values, -3.0, 3.0) * scale


def draw_candidates(key, part):
    offset = shared_offset(key)
    half_width = math.sqrt(12.0 / DIN)
    spread = jax.random.uniform(jax.random.fold_in(key, 104), (DIN, CANDS), jnp.float32, -half_width, half_width)
    return offset[:, None] + spread


def place_ends(values, stream_key, smallest, top_value):
    longest = values.shape.index(max(values.shape))
    spots = []
    for shift in (0, 1):
        where = [jax.random.randint(jax.random.fold_in(stream_key, axis), (), 0, length) for axis, length in enumerate(values.shape)]
        where[longest] = (where[longest] + shift) % values.shape[longest]
        spots.append(tuple(where))
    return values.at[spots[0]].set(smallest).at[spots[1]].set(top_value)


def levels(stream_key, shape, split, smallest, largest):
    def one(dim, shards_of):
        heights = jax.random.uniform(jax.random.fold_in(jax.random.fold_in(stream_key, 6), dim), (shards_of,), jnp.float32, smallest / len(split), largest / len(split))
        return jnp.repeat(jnp.exp(heights), shape[dim] // shards_of).reshape((-1,) + (1,) * (len(shape) - dim - 1))

    loudness = one(*split[0])
    for cut in split[1:]:
        loudness = loudness * one(*cut)
    return loudness


def noise(stream_key, dims, width, most, pieces=(), held_as=jnp.bfloat16):
    result = width * jax.random.normal(stream_key, dims, jnp.float32)
    if pieces:
        result = result * levels(stream_key, dims, pieces, -0.22, 0.18)
    return jnp.clip(result, -most, most).astype(held_as)


def setup_inputs(seed: int = 0) -> dict:
    key_list = jax.random.split(jax.random.key(seed), 8)
    return {
        "train_inputs": draw_train_inputs(jax.random.fold_in(key_list[7], 71), 0),
        "inv_factor": draw_inv_factor(jax.random.fold_in(key_list[7], 71), 0),
        "weights": draw_weights(jax.random.fold_in(key_list[7], 71), 0),
        "candidates": draw_candidates(jax.random.fold_in(key_list[7], 71), 0),
        "test_ids": place_ends(jax.random.randint(key_list[4], (TESTS,), 0, CANDS), jax.random.fold_in(key_list[4], 1), 0, CANDS - 1).astype(jnp.int32),
        "basis": noise(key_list[5], (OUT, CELLS), OUT ** -0.5, 0.25, ((1, 256),)),
        "climatology": noise(key_list[6], (CELLS,), 0.5, 3.0, ((0, 256),), jnp.float32),
    }


signal_var = 1.0
noise_var = 0.1

def cross_cov(train_points, query_points):
    sq_train = jnp.sum(train_points * train_points, axis=0)
    sq_query = jnp.sum(query_points * query_points, axis=0)
    inner = lax.dot_general(train_points.astype(jnp.float32), query_points.astype(jnp.float32), (((0,), (0,)), ((), ())), precision=lax.Precision.HIGHEST, preferred_element_type=jnp.float32)
    return signal_var * jnp.exp(-0.5 * (sq_train[:, None] + sq_query[None, :] - 2.0 * inner))

def expert_terms(train_points, factor, expert_weights, query_points):
    cross_kernel = cross_cov(train_points, query_points)
    expert_mean = lax.dot_general(cross_kernel.astype(jnp.float32), expert_weights.astype(jnp.float32), (((0,), (0,)), ((), ())), precision=lax.Precision.HIGHEST, preferred_element_type=jnp.float32)
    whitened = jnp.dot(factor.astype(jnp.float32), cross_kernel.astype(jnp.float32), precision=lax.Precision.HIGHEST, preferred_element_type=jnp.float32)
    explained = jnp.sum(whitened * whitened, axis=0)
    prior_var = signal_var + noise_var
    post_var = prior_var - explained
    beta_weight = 0.5 * (jnp.log(prior_var) - jnp.log(post_var))
    precision_term = beta_weight / post_var
    return (expert_mean * precision_term[:, None], precision_term, beta_weight)

def reference(train_inputs, inv_factor, weights, candidates, test_ids, basis, climatology):
    query_points = jnp.take(candidates, test_ids.astype(jnp.int32), axis=1)

    def accumulate(carry, items):
        partial_value, weight_term, beta_weight = expert_terms(items[0], items[1], items[2], query_points)
        return ((carry[0] + partial_value, carry[1] + weight_term, carry[2] + beta_weight), None)
    start = (jnp.zeros((TESTS, OUT), jnp.float32), jnp.zeros((TESTS,), jnp.float32), jnp.zeros((TESTS,), jnp.float32))
    sums, _ = lax.scan(accumulate, start, (train_inputs, inv_factor, weights))
    mean_total, weight_total, beta_total = sums
    precision = weight_total + (1.0 - beta_total) / (signal_var + noise_var)
    coefficients = (mean_total / precision[:, None]).astype(jnp.bfloat16)
    nblocks = CELLS // CELL_DEV
    basis_blocks = basis.reshape(OUT, nblocks, CELL_DEV).transpose(1, 0, 2)
    clim_blocks = climatology.reshape(nblocks, CELL_DEV)

    def reconstruct(items):
        field_sum = jnp.dot(coefficients.astype(jnp.float32), items[0].astype(jnp.float32), preferred_element_type=jnp.float32) + items[1][None, :]
        return field_sum.astype(jnp.bfloat16)
    blocks = lax.map(reconstruct, (basis_blocks, clim_blocks))
    return blocks.transpose(1, 0, 2).reshape(TESTS, CELLS)
```

```python
import functools

import jax
import jax.numpy as jnp
from jax import lax
from jax.experimental import pallas as pl
from jax.experimental.pallas import tpu as pltpu
from jax.sharding import PartitionSpec as P

MESH = pl.DeviceIdType.MESH
F32, BF16 = jnp.float32, jnp.bfloat16
PRIOR_VAR = 1.1
TB = 256


def split3(a):
    hi = a.astype(BF16)
    rest = a - hi.astype(F32)
    mid = rest.astype(BF16)
    low = (rest - mid.astype(F32)).astype(BF16)
    return hi, mid, low


def gather_queries(cand_ref, ids_ref, query_ref):
    for tb in range(8):
        ids = jnp.broadcast_to(ids_ref[tb : tb + 1, :], (8, 128))
        lane, block = ids & 127, ids >> 7
        for half in range(2):
            rows = slice(half * 8, half * 8 + 8)
            got = jnp.zeros((8, 128), F32)
            for h in range(32):
                values = jnp.take_along_axis(
                    cand_ref[rows, h * 128 : h * 128 + 128], lane, axis=1, mode="promise_in_bounds"
                )
                got = jnp.where(block == h, values, got)
            query_ref[rows, tb * 128 : tb * 128 + 128] = got


def exponent_sides(query, train):
    qh, qm, ql = split3(query)
    xh, xm, xl = split3(train)
    t = split3(-0.5 * jnp.sum(query * query, axis=0, keepdims=True))
    s = split3(-0.5 * jnp.sum(train * train, axis=0, keepdims=True))
    row = lax.broadcasted_iota(jnp.int32, query.shape, 0)

    def rows(first, parts):
        out = jnp.zeros(query.shape, F32)
        for i, part in enumerate(parts):
            out = jnp.where(row == first + i, part.astype(F32), out)
        return out

    ones = lambda first: jnp.where((row >= first) & (row < first + 3), 1.0, 0.0)
    zero = jnp.zeros(query.shape, BF16)
    left = [qh, qh, qm, qm, qh, ql, (rows(0, t) + ones(3)).astype(BF16), zero]
    right = [xh, xm, xh, xm, xl, xh, (rows(3, s) + ones(0)).astype(BF16), zero]
    return jnp.concatenate(left, 0), jnp.concatenate(right, 0)


def dot_nt(a, b):
    return lax.dot_general(a, b, (((1,), (1,)), ((), ())), preferred_element_type=F32)


def expert_kernel(train_ref, factor_ref, weights_ref, cand_ref, ids_ref, part_ref, q_ref, query_ref, left_ref, right_ref, lb_ref, ll_ref, wb_ref):
    gather_queries(cand_ref, ids_ref, query_ref)
    left, right = exponent_sides(query_ref[...], train_ref[...])
    left_ref[...] = left.T
    right_ref[...] = right
    for b in range(4):
        block = slice(b * 256, b * 256 + 256), slice(0, 256 * (b + 1))
        factor = factor_ref[block]
        high = factor.astype(BF16)
        lb_ref[block] = high
        ll_ref[block] = (factor - high.astype(F32)).astype(BF16)
    wb_ref[...] = weights_ref[...].astype(BF16)
    eye = lax.broadcasted_iota(jnp.int32, (128, 128), 0) == lax.broadcasted_iota(jnp.int32, (128, 128), 1)
    for tb in range(1024 // TB):
        kernel = jnp.exp(jnp.dot(left_ref[tb * TB : tb * TB + TB, :], right_ref[...], preferred_element_type=F32))
        kt = kernel.astype(BF16)
        kl = (kernel - kt.astype(F32)).astype(BF16)
        explained = jnp.zeros((TB, 1), F32)
        for b in range(4):
            block = slice(b * 256, b * 256 + 256), slice(0, 256 * (b + 1))
            whitened = dot_nt(kt[:, block[1]], lb_ref[block])
            whitened += dot_nt(kl[:, block[1]], lb_ref[block])
            whitened += dot_nt(kt[:, block[1]], ll_ref[block])
            explained += jnp.sum(whitened * whitened, axis=1, keepdims=True)
        post_var = PRIOR_VAR - explained
        beta = 0.5 * (jnp.log(jnp.full_like(post_var, PRIOR_VAR)) - jnp.log(post_var))
        term = beta / post_var
        q = term - beta / PRIOR_VAR
        mean = jnp.dot(kt, wb_ref[...], preferred_element_type=F32) * term
        for cb in range(4):
            part_ref[tb * TB // 16 : (tb + 1) * TB // 16, cb] = mean[:, cb * 128 : cb * 128 + 128].reshape(TB // 16, 16, 128)
        for i in range(TB // 128):
            lanes = jnp.sum(jnp.where(eye, q[i * 128 : i * 128 + 128], 0.0), axis=0, keepdims=True)
            q_ref[tb * (TB // 128) + i : tb * (TB // 128) + i + 1, :] = lanes


def place():
    group, expert = lax.axis_index("group"), lax.axis_index("expert")
    return group // 8, group % 8, expert // 4, (expert // 2) % 2, expert % 2


def device(x, y, z, core):
    return ((y % 2) * 8 + z, x * 4 + (y // 2) * 2 + core)


def split_q(q):
    hi = q.astype(BF16).astype(F32)
    return jnp.concatenate([hi, q - hi], 0).astype(BF16)


def join_q(tile):
    tile = tile.astype(F32)
    return tile[:8] + tile[8:]


def sum_kernel(part_ref, q_ref, out_ref, c_recv, x_sum, x_send, x_recv, y_sum, y_recv, z_sum, z_recv,
               tq_send, tq_recv, s_send, s_recv, q_s, q_r, g_s, g_r):
    y_lo, z, x, y_hi, core = place()
    y = y_hi * 2 + y_lo
    peers = (
        [device(x, y, z, 1 - core)]
        + [device((x + d) % 4, y, z, core) for d in (1, 2, 3)]
        + [device(x, (y + d) % 4, z, core) for d in (1, 2, 3)]
        + [device(x, y, (z + d) % 8, core) for d in range(1, 8)]
    )
    barrier = pltpu.get_barrier_semaphore()
    for peer in peers:
        pl.semaphore_signal(barrier, inc=1, device_id=peer, device_id_type=MESH)
    pl.semaphore_wait(barrier, len(peers))

    def send(k, src, dst, gather=False):
        copy = pltpu.make_async_remote_copy(
            src_ref=src, dst_ref=dst,
            send_sem=(g_s if gather else s_send).at[k], recv_sem=(g_r if gather else s_recv).at[k],
            device_id=peers[k], device_id_type=MESH,
        )
        copy.start()
        return copy

    def send_q(k, stage):
        copy = pltpu.make_async_remote_copy(
            src_ref=tq_send.at[stage], dst_ref=tq_recv.at[k], send_sem=q_s.at[k], recv_sem=q_r.at[k],
            device_id=peers[k], device_id_type=MESH,
        )
        copy.start()
        return copy

    started = []
    q = q_ref[...]
    tq_send[0] = split_q(q)
    copies = [send(0, part_ref.at[pl.ds((1 - core) * 32, 32)], c_recv), send_q(0, 0)]
    for c in copies:
        c.wait()
    q += join_q(tq_recv[0])
    x_sum[...] = part_ref[pl.ds(core * 32, 32)] + c_recv[...]

    x_send[...] = x_sum[...].astype(BF16)
    tq_send[1] = split_q(q)
    copies = []
    for i in range(3):
        copies += [send(1 + i, x_send.at[pl.ds(((x + 1 + i) % 4) * 8, 8)], x_recv.at[i]), send_q(1 + i, 1)]
    for c in copies:
        c.wait()
    total = x_sum[pl.ds(x * 8, 8)]
    for i in range(3):
        total += x_recv[i].astype(F32)
        q += join_q(tq_recv[1 + i])
    y_sum[...] = total

    tq_send[2] = split_q(q)
    copies = []
    for i in range(3):
        copies += [send(4 + i, y_sum.at[pl.ds(((y + 1 + i) % 4) * 2, 2)], y_recv.at[i]), send_q(4 + i, 2)]
    for c in copies:
        c.wait()
    total = y_sum[pl.ds(y * 2, 2)]
    for i in range(3):
        total += y_recv[i]
        q += join_q(tq_recv[4 + i])
    z_sum[...] = total

    tq_send[3] = split_q(q)
    copies = []
    for i in range(7):
        to = (z + 1 + i) % 8
        copies += [send(7 + i, z_sum.at[to // 4, to % 4], z_recv.at[i]), send_q(7 + i, 3)]
    for c in copies:
        c.wait()
    total = z_sum[z // 4, z % 4]
    for i in range(7):
        total += z_recv[i]
        q += join_q(tq_recv[7 + i])

    precision = q + 1.0 / PRIOR_VAR
    row = lax.broadcasted_iota(jnp.int32, (8, 128), 0)
    line = jnp.sum(jnp.where(row == core * 4 + x, precision, 0.0), axis=0, keepdims=True)
    pick = lax.broadcasted_iota(jnp.int32, (16, 128), 1) == lax.broadcasted_iota(jnp.int32, (16, 128), 0) + (y * 32 + (z // 4) * 16)
    column = jnp.sum(jnp.where(pick, line, 0.0), axis=1, keepdims=True)

    base_x = (core * 4 + x) * 8
    base_y = base_x + y * 2
    out_ref[base_y + z // 4, z % 4] = (total / column).astype(BF16)
    mine = out_ref.at[base_y + z // 4, z % 4]
    copies = [send(7 + i, mine, mine, True) for i in range(7)]
    for c in copies:
        c.wait()
    mine = out_ref.at[pl.ds(base_y, 2)]
    copies = [send(4 + i, mine, mine, True) for i in range(3)]
    for c in copies:
        c.wait()
    mine = out_ref.at[pl.ds(base_x, 8)]
    copies = [send(1 + i, mine, mine, True) for i in range(3)]
    for c in copies:
        c.wait()
    mine = out_ref.at[pl.ds(core * 32, 32)]
    send(0, mine, mine, True).wait()


def field_kernel(coef_ref, basis_ref, clim_ref, out_ref):
    rows = out_ref.shape[0]
    coef = jnp.concatenate([coef_ref[:, cb].reshape(rows, 128) for cb in range(4)], axis=1)
    out_ref[...] = (jnp.dot(coef, basis_ref[...], preferred_element_type=F32) + clim_ref[...]).astype(BF16)


VM = pl.BlockSpec(memory_space=pltpu.VMEM)


def body(train_inputs, inv_factor, weights, candidates, test_ids, basis, climatology):
    part, q = pl.pallas_call(
        expert_kernel,
        out_shape=(jax.ShapeDtypeStruct((64, 4, 16, 128), F32), jax.ShapeDtypeStruct((8, 128), F32)),
        in_specs=[VM] * 5,
        out_specs=(VM, VM),
        scratch_shapes=[
            pltpu.VMEM((16, 1024), F32),
            pltpu.VMEM((1024, 128), BF16),
            pltpu.VMEM((128, 1024), BF16),
            pltpu.VMEM((1024, 1024), BF16),
            pltpu.VMEM((1024, 1024), BF16),
            pltpu.VMEM((1024, 512), BF16),
        ],
        compiler_params=pltpu.CompilerParams(vmem_limit_bytes=40 << 20),
    )(train_inputs[0], inv_factor[0], weights[0], candidates, test_ids.reshape(8, 128))
    dma = pltpu.SemaphoreType.DMA
    coef = pl.pallas_call(
        sum_kernel,
        out_shape=jax.ShapeDtypeStruct((64, 4, 16, 128), BF16),
        in_specs=[VM] * 2,
        out_specs=VM,
        scratch_shapes=[
            pltpu.VMEM((32, 4, 16, 128), F32),
            pltpu.VMEM((32, 4, 16, 128), F32), pltpu.VMEM((32, 4, 16, 128), BF16), pltpu.VMEM((3, 8, 4, 16, 128), BF16),
            pltpu.VMEM((8, 4, 16, 128), F32), pltpu.VMEM((3, 2, 4, 16, 128), F32),
            pltpu.VMEM((2, 4, 16, 128), F32), pltpu.VMEM((7, 16, 128), F32),
            pltpu.VMEM((4, 16, 128), BF16), pltpu.VMEM((14, 16, 128), BF16),
            dma((14,)), dma((14,)), dma((14,)), dma((14,)), dma((14,)), dma((14,)),
        ],
        compiler_params=pltpu.CompilerParams(collective_id=0, has_side_effects=True, vmem_limit_bytes=24 << 20),
    )(part, q)
    return pl.pallas_call(
        field_kernel,
        out_shape=jax.ShapeDtypeStruct((1024, 1024), BF16),
        grid=(4,),
        in_specs=[
            pl.BlockSpec((16, 4, 16, 128), lambda i: (i, 0, 0, 0)),
            pl.BlockSpec((512, 1024), lambda i: (0, 0)),
            pl.BlockSpec((1, 1024), lambda i: (0, 0)),
        ],
        out_specs=pl.BlockSpec((256, 1024), lambda i: (i, 0)),
        compiler_params=pltpu.CompilerParams(vmem_limit_bytes=24 << 20),
    )(coef, basis, climatology.reshape(1, 1024))


def solution(mesh):
    both = ("group", "expert")
    return jax.shard_map(
        body,
        mesh=mesh,
        in_specs=(P(both, None, None), P(both, None, None), P(both, None, None), P(), P(), P(None, both), P(both)),
        out_specs=P(None, both),
        check_vma=False,
    )
```

```python
import functools

import jax
import jax.numpy as jnp
from jax import lax
from jax.experimental import pallas as pl
from jax.experimental.pallas import tpu as pltpu
from jax.sharding import PartitionSpec as P

MESH = pl.DeviceIdType.MESH
F32, BF16 = jnp.float32, jnp.bfloat16
PRIOR_VAR = 1.1
TB = 256
PLANE = [(dx, dy) for dx in range(4) for dy in range(4) if dx or dy]
PLANE.sort(key=lambda d: -(min(d[0], 4 - d[0]) + min(d[1], 4 - d[1])))
ALONG = [4, 3, 5, 2, 6, 1, 7]


def split3(a):
    hi = a.astype(BF16)
    rest = a - hi.astype(F32)
    mid = rest.astype(BF16)
    low = (rest - mid.astype(F32)).astype(BF16)
    return hi, mid, low


def gather_queries(cand_ref, ids_ref, query_ref):
    for tb in range(8):
        ids = jnp.broadcast_to(ids_ref[tb : tb + 1, :], (8, 128))
        lane, block = ids & 127, ids >> 7
        for half in range(2):
            rows = slice(half * 8, half * 8 + 8)
            got = jnp.zeros((8, 128), F32)
            for h in range(32):
                values = jnp.take_along_axis(
                    cand_ref[rows, h * 128 : h * 128 + 128], lane, axis=1, mode="promise_in_bounds"
                )
                got = jnp.where(block == h, values, got)
            query_ref[rows, tb * 128 : tb * 128 + 128] = got


def exponent_sides(query, train):
    qh, qm, ql = split3(query)
    xh, xm, xl = split3(train)
    t = split3(-0.5 * jnp.sum(query * query, axis=0, keepdims=True))
    s = split3(-0.5 * jnp.sum(train * train, axis=0, keepdims=True))
    row = lax.broadcasted_iota(jnp.int32, query.shape, 0)

    def rows(first, parts):
        out = jnp.zeros(query.shape, F32)
        for i, part in enumerate(parts):
            out = jnp.where(row == first + i, part.astype(F32), out)
        return out

    ones = lambda first: jnp.where((row >= first) & (row < first + 3), 1.0, 0.0)
    zero = jnp.zeros(query.shape, BF16)
    left = [qh, qh, qm, qm, qh, ql, (rows(0, t) + ones(3)).astype(BF16), zero]
    right = [xh, xm, xh, xm, xl, xh, (rows(3, s) + ones(0)).astype(BF16), zero]
    return jnp.concatenate(left, 0), jnp.concatenate(right, 0)


def dot_nt(a, b):
    return lax.dot_general(a, b, (((1,), (1,)), ((), ())), preferred_element_type=F32)


def place():
    group, expert = lax.axis_index("group"), lax.axis_index("expert")
    return group // 8, group % 8, expert // 4, (expert // 2) % 2, expert % 2


def device(x, y, z, core):
    return ((y % 2) * 8 + z, x * 4 + (y // 2) * 2 + core)


def split_q(q):
    hi = q.astype(BF16).astype(F32)
    return jnp.concatenate([hi, q - hi], 0).astype(BF16)


def join_q(tile):
    tile = tile.astype(F32)
    return tile[:8] + tile[8:]


def tiles(a):
    return jnp.stack([a[:, cb * 128 : cb * 128 + 128].reshape(-1, 16, 128) for cb in range(4)], axis=1)


def rows_of(t):
    return jnp.concatenate([t[:, cb].reshape(-1, 128) for cb in range(4)], axis=1)


def main_kernel(train_hbm, cand_hbm, ids_hbm, factor_ref, weights_ref, basis_ref, clim_hbm, out_ref,
                train_ref, cand_ref, ids_ref, query_ref, left_ref, right_ref, lf, lb, ll, wf, wb, basis_v, clim_ref, kh, kl, term_ref, q_ref,
                c_send, c_recv, own, p_send0, p_send1, p_recv0, p_recv1, z_send, z_recv, z_own, coef,
                i_sem, l_sem, w_sem, b_sem, m_sem, c_s, c_r, p_s, p_r, z_s, z_r, g_s, g_r, h_s, h_r):
    y_lo, z, x, y_hi, core = place()
    y = y_hi * 2 + y_lo
    plane = x * 4 + y
    partner = device(x, y, z, 1 - core)
    plane_peers = [device((x + dx) % 4, (y + dy) % 4, z, core) for dx, dy in PLANE]
    z_peers = [device(x, y, (z + d) % 8, core) for d in ALONG]

    copies = [
        pltpu.make_async_copy(ids_hbm, ids_ref, i_sem.at[0]),
        pltpu.make_async_copy(cand_hbm, cand_ref, i_sem.at[1]),
        pltpu.make_async_copy(train_hbm, train_ref, i_sem.at[2]),
    ]
    for copy in copies:
        copy.start()
    l_copies = []
    for b in range(4):
        block = pl.ds(b * 256, 256), pl.ds(0, 256 * (b + 1))
        l_copies.append(pltpu.make_async_copy(factor_ref.at[block], lf.at[block], l_sem.at[b]))
    w_copy = pltpu.make_async_copy(weights_ref, wf, w_sem)
    m_copy = pltpu.make_async_copy(clim_hbm, clim_ref, m_sem)
    b_copy = pltpu.make_async_copy(basis_ref, basis_v, b_sem)
    for copy in l_copies:
        copy.start()
    w_copy.start()
    b_copy.start()
    m_copy.start()

    barrier = pltpu.get_barrier_semaphore()
    everyone = [partner] + plane_peers + z_peers
    for peer in everyone:
        pl.semaphore_signal(barrier, inc=1, device_id=peer, device_id_type=MESH)

    def send(src, dst, s_sem, r_sem, peer):
        copy = pltpu.make_async_remote_copy(
            src_ref=src, dst_ref=dst, send_sem=s_sem, recv_sem=r_sem, device_id=peer, device_id_type=MESH
        )
        copy.start()
        return copy

    for copy in copies:
        copy.wait()
    gather_queries(cand_ref, ids_ref, query_ref)
    left, right = exponent_sides(query_ref[...], train_ref[...])
    left_ref[...] = left.T
    right_ref[...] = right

    @pl.loop(0, 4)
    def _(tb):
        rows = pl.ds(pl.multiple_of(tb * TB, TB), TB)
        kernel = jnp.exp(jnp.dot(left_ref[rows, :], right_ref[...], preferred_element_type=F32))
        high = kernel.astype(BF16)
        kh[rows, :] = high
        kl[rows, :] = (kernel - high.astype(F32)).astype(BF16)

    for b in range(4):
        l_copies[b].wait()
        block = slice(b * 256, b * 256 + 256), slice(0, 256 * (b + 1))
        factor = lf[block]
        high = factor.astype(BF16)
        lb[block] = high
        ll[block] = (factor - high.astype(F32)).astype(BF16)

    eye = lax.broadcasted_iota(jnp.int32, (128, 128), 0) == lax.broadcasted_iota(jnp.int32, (128, 128), 1)

    @pl.loop(0, 4)
    def _(tb):
        rows = pl.ds(pl.multiple_of(tb * TB, TB), TB)
        explained = jnp.zeros((TB, 1), F32)
        for b in range(4):
            block = slice(b * 256, b * 256 + 256), slice(0, 256 * (b + 1))
            whitened = dot_nt(kh[rows, block[1]], lb[block])
            whitened += dot_nt(kl[rows, block[1]], lb[block])
            whitened += dot_nt(kh[rows, block[1]], ll[block])
            explained += jnp.sum(whitened * whitened, axis=1, keepdims=True)
        post_var = PRIOR_VAR - explained
        beta = 0.5 * (jnp.log(jnp.full_like(post_var, PRIOR_VAR)) - jnp.log(post_var))
        term = beta / post_var
        term_ref[rows, :] = term
        q = term - beta / PRIOR_VAR
        for i in range(TB // 128):
            lanes = jnp.sum(jnp.where(eye, q[i * 128 : i * 128 + 128], 0.0), axis=0, keepdims=True)
            q_ref[pl.ds(tb * (TB // 128) + i, 1), :] = lanes

    w_copy.wait()
    wb[...] = wf[...].astype(BF16)

    def mean(block):
        rows = pl.ds(pl.multiple_of(block * TB, TB), TB)
        return tiles(jnp.dot(kh[rows, :], wb[...], preferred_element_type=F32) * term_ref[rows, :])

    q = q_ref[...]
    c_send[0, 64, :8] = q
    c_send[0, 64, 8:] = q
    core_copies = []
    for g in range(2):
        c_send[g, :64] = mean(g * 2 + 1 - core).reshape(64, 16, 128)
        if g == 0:
            pl.semaphore_wait(barrier, len(everyone))
        n = 65 if g == 0 else 64
        core_copies.append(send(c_send.at[g, pl.ds(0, n)], c_recv.at[g, pl.ds(0, n)], c_s.at[g], c_r.at[g], partner))

    plane_copies = [[], []]
    for g in range(2):
        mine = mean(g * 2 + core)
        core_copies[g].wait()
        mine += c_recv[g, :64].reshape(16, 4, 16, 128)
        own[g] = mine
        p_send, p_recv = (p_send0, p_recv0) if g == 0 else (p_send1, p_recv1)
        p_send[:, :4] = mine.astype(BF16)
        if g == 0:
            q += c_recv[0, 64, :8]
            p_send[:, 4] = jnp.broadcast_to(split_q(q)[None], (16, 16, 128))
        for k, (dx, dy) in enumerate(PLANE):
            to = ((x + dx) % 4) * 4 + (y + dy) % 4
            plane_copies[g].append(send(p_send.at[to], p_recv.at[k], p_s.at[g, k], p_r.at[g, k], plane_peers[k]))

    z_copies = [[], []]
    for g in range(2):
        p_recv = p_recv0 if g == 0 else p_recv1
        total = own[g, plane]
        for k in range(15):
            plane_copies[g][k].wait()
            total += p_recv[k, :4].astype(F32)
            if g == 0:
                q += join_q(p_recv[k, 4])
        z_own[g] = total
        z_send[g, :4] = total.astype(BF16)
        if g == 0:
            z_send[0, 4] = split_q(q)
        n = 5 if g == 0 else 4
        for k in range(7):
            z_copies[g].append(send(z_send.at[g, pl.ds(0, n)], z_recv.at[g, k, pl.ds(0, n)], z_s.at[g, k], z_r.at[g, k], z_peers[k]))

    row = lax.broadcasted_iota(jnp.int32, (8, 128), 0)
    pick_row = lax.broadcasted_iota(jnp.int32, (16, 128), 0) + (plane % 8) * 16
    pick = lax.broadcasted_iota(jnp.int32, (16, 128), 1) == pick_row
    gather_copies = [[], []]
    for g in range(2):
        total = z_own[g]
        for k in range(7):
            z_copies[g][k].wait()
            total += z_recv[g, k, :4].astype(F32)
            if g == 0:
                q += join_q(z_recv[0, k, 4])
        if g == 0:
            precision = q + 1.0 / PRIOR_VAR
        line = jnp.sum(jnp.where(row == (g * 2 + core) * 2 + plane // 8, precision, 0.0), axis=0, keepdims=True)
        column = jnp.sum(jnp.where(pick, line, 0.0), axis=1, keepdims=True)
        spot = (g * 2 + core) * 16 + plane
        coef[spot] = (total / column).astype(BF16)
        for k in range(15):
            gather_copies[g].append(send(coef.at[spot], coef.at[spot], g_s.at[g, k], g_r.at[g, k], plane_peers[k]))

    b_copy.wait()
    m_copy.wait()

    def field(block):
        c = rows_of(coef[pl.ds(block * 16, 16)])
        rows = pl.ds(pl.multiple_of(block * TB, TB), TB)
        out_ref[rows, :] = (jnp.dot(c, basis_v[...], preferred_element_type=F32) + clim_ref[...]).astype(BF16)

    last = []
    for g in range(2):
        for k in range(15):
            gather_copies[g][k].wait()
        half = coef.at[pl.ds((g * 2 + core) * 16, 16)]
        last.append(send(half, half, h_s.at[g], h_r.at[g], partner))
    field(core)
    last[0].wait()
    field(1 - core)
    field(2 + core)
    last[1].wait()
    field(3 - core)


VM = pl.BlockSpec(memory_space=pltpu.VMEM)
HBM = pl.BlockSpec(memory_space=pltpu.HBM)


def body(train_inputs, inv_factor, weights, candidates, test_ids, basis, climatology):
    arrays = train_inputs[0], candidates, test_ids.reshape(8, 128), inv_factor[0], weights[0], basis, climatology.reshape(1, 1024)
    dma = pltpu.SemaphoreType.DMA
    tile = lambda *n: pltpu.VMEM((*n, 16, 128), BF16)
    tile32 = lambda *n: pltpu.VMEM((*n, 16, 128), F32)
    return pl.pallas_call(
        main_kernel,
        out_shape=jax.ShapeDtypeStruct((1024, 1024), BF16),
        in_specs=[HBM] * 7,
        out_specs=VM,
        scratch_shapes=[
            pltpu.VMEM((16, 1024), F32), pltpu.VMEM((16, 4096), F32), pltpu.VMEM((8, 128), jnp.int32), pltpu.VMEM((16, 1024), F32),
            pltpu.VMEM((1024, 128), BF16), pltpu.VMEM((128, 1024), BF16),
            pltpu.VMEM((1024, 1024), F32), pltpu.VMEM((1024, 1024), BF16), pltpu.VMEM((1024, 1024), BF16),
            pltpu.VMEM((1024, 512), F32), pltpu.VMEM((1024, 512), BF16), pltpu.VMEM((512, 1024), BF16), pltpu.VMEM((1, 1024), F32),
            pltpu.VMEM((1024, 1024), BF16), pltpu.VMEM((1024, 1024), BF16),
            pltpu.VMEM((1024, 1), F32), pltpu.VMEM((8, 128), F32),
            tile32(2, 65), tile32(2, 65), tile32(2, 16, 4),
            tile(16, 5), tile(16, 4), tile(15, 5), tile(15, 4), tile(2, 5), tile(2, 7, 5), tile32(2, 4), tile(64, 4),
            dma((3,)), dma((4,)), dma, dma, dma, dma((2,)), dma((2,)), dma((2, 15)), dma((2, 15)), dma((2, 7)), dma((2, 7)),
            dma((2, 15)), dma((2, 15)), dma((2,)), dma((2,)),
        ],
        compiler_params=pltpu.CompilerParams(collective_id=0, has_side_effects=True, vmem_limit_bytes=44 << 20),
    )(*[pltpu.with_memory_space_constraint(a, pltpu.HBM) for a in arrays])


def solution(mesh):
    both = ("group", "expert")
    return jax.shard_map(
        body,
        mesh=mesh,
        in_specs=(P(both, None, None), P(both, None, None), P(both, None, None), P(), P(), P(None, both), P(both)),
        out_specs=P(None, both),
        check_vma=False,
    )
```

```python
import functools

import jax
import jax.numpy as jnp
from jax import lax
from jax.experimental import pallas as pl
from jax.experimental.pallas import tpu as pltpu
from jax.sharding import PartitionSpec as P

MESH = pl.DeviceIdType.MESH
F32, BF16 = jnp.float32, jnp.bfloat16
PRIOR_VAR = 1.1
NK = 2
PLANE = [(dx, dy) for dx in range(4) for dy in range(4) if dx or dy]
PLANE.sort(key=lambda d: -(min(d[0], 4 - d[0]) + min(d[1], 4 - d[1])))
ALONG = [4, 3, 5, 2, 6, 1, 7]


def split3(a):
    hi = a.astype(BF16)
    rest = a - hi.astype(F32)
    mid = rest.astype(BF16)
    low = (rest - mid.astype(F32)).astype(BF16)
    return hi, mid, low


def gather_queries(cand_ref, ids_ref, query_ref):
    for tb in range(8):
        ids = jnp.broadcast_to(ids_ref[tb : tb + 1, :], (8, 128))
        lane, block = ids & 127, ids >> 7
        for half in range(2):
            rows = slice(half * 8, half * 8 + 8)
            got = jnp.zeros((8, 128), F32)
            for h in range(32):
                values = jnp.take_along_axis(
                    cand_ref[rows, h * 128 : h * 128 + 128], lane, axis=1, mode="promise_in_bounds"
                )
                got = jnp.where(block == h, values, got)
            query_ref[rows, tb * 128 : tb * 128 + 128] = got


def exponent_sides(query, train):
    qh, qm, ql = split3(query)
    xh, xm, xl = split3(train)
    t = split3(-0.5 * jnp.sum(query * query, axis=0, keepdims=True))
    s = split3(-0.5 * jnp.sum(train * train, axis=0, keepdims=True))
    row = lax.broadcasted_iota(jnp.int32, query.shape, 0)

    def rows(first, parts):
        out = jnp.zeros(query.shape, F32)
        for i, part in enumerate(parts):
            out = jnp.where(row == first + i, part.astype(F32), out)
        return out

    ones = lambda first: jnp.where((row >= first) & (row < first + 3), 1.0, 0.0)
    zero = jnp.zeros(query.shape, BF16)
    left = [qh, qh, qm, qm, qh, ql, (rows(0, t) + ones(3)).astype(BF16), zero]
    right = [xh, xm, xh, xm, xl, xh, (rows(3, s) + ones(0)).astype(BF16), zero]
    return jnp.concatenate(left, 0), jnp.concatenate(right, 0)


def dot_nt(a, b):
    return lax.dot_general(a, b, (((1,), (1,)), ((), ())), preferred_element_type=F32)


def place():
    group, expert = lax.axis_index("group"), lax.axis_index("expert")
    return group // 8, group % 8, expert // 4, (expert // 2) % 2, expert % 2


def device(x, y, z, core):
    return ((y % 2) * 8 + z, x * 4 + (y // 2) * 2 + core)


def split_q(q):
    hi = q.astype(BF16).astype(F32)
    return jnp.concatenate([hi, q - hi], 0).astype(BF16)


def join_q(tile):
    tile = tile.astype(F32)
    return tile[:8] + tile[8:]


def tiles(a):
    return jnp.stack([a[:, cb * 128 : cb * 128 + 128].reshape(-1, 16, 128) for cb in range(4)], axis=1)


def rows_of(t):
    return jnp.concatenate([t[:, cb].reshape(-1, 128) for cb in range(4)], axis=1)


def main_kernel(train_hbm, cand_hbm, ids_hbm, factor_ref, weights_ref, basis_ref, clim_hbm, out_ref,
                train_ref, cand_ref, ids_ref, query_ref, left_ref, right_ref, lf, lb, ll, wf, wb, basis_v, clim_ref, kh, kl, term_ref, q_ref,
                c_send, c_recv, own, p_send0, p_send, p_recv0, p_recv, z_send, z_recv0, z_recv, z_own, coef,
                i_sem, l_sem, w_sem, b_sem, m_sem, c_s, c_r, p_s, p_r, z_s, z_r, g_s, g_r, h_s, h_r):
    y_lo, z, x, y_hi, core = place()
    y = y_hi * 2 + y_lo
    plane = x * 4 + y
    partner = device(x, y, z, 1 - core)
    plane_peers = [device((x + dx) % 4, (y + dy) % 4, z, core) for dx, dy in PLANE]
    z_peers = [device(x, y, (z + d) % 8, core) for d in ALONG]

    copies = [
        pltpu.make_async_copy(ids_hbm, ids_ref, i_sem.at[0]),
        pltpu.make_async_copy(cand_hbm, cand_ref, i_sem.at[1]),
        pltpu.make_async_copy(train_hbm, train_ref, i_sem.at[2]),
    ]
    for copy in copies:
        copy.start()
    l_copies = []
    for b in range(4):
        block = pl.ds(b * 256, 256), pl.ds(0, 256 * (b + 1))
        l_copies.append(pltpu.make_async_copy(factor_ref.at[block], lf.at[block], l_sem.at[b]))
    w_copy = pltpu.make_async_copy(weights_ref, wf, w_sem)
    m_copy = pltpu.make_async_copy(clim_hbm, clim_ref, m_sem)
    b_copy = pltpu.make_async_copy(basis_ref, basis_v, b_sem)
    for copy in l_copies:
        copy.start()

    barrier = pltpu.get_barrier_semaphore()
    everyone = [partner] + plane_peers + z_peers
    for peer in everyone:
        pl.semaphore_signal(barrier, inc=1, device_id=peer, device_id_type=MESH)

    def send(src, dst, s_sem, r_sem, peer):
        copy = pltpu.make_async_remote_copy(
            src_ref=src, dst_ref=dst, send_sem=s_sem, recv_sem=r_sem, device_id=peer, device_id_type=MESH
        )
        copy.start()
        return copy

    def wait_all(like, s_sem, r_sem, peer):
        pltpu.make_async_remote_copy(
            src_ref=like, dst_ref=like, send_sem=s_sem, recv_sem=r_sem, device_id=peer, device_id_type=MESH
        ).wait()

    for copy in copies:
        copy.wait()
    gather_queries(cand_ref, ids_ref, query_ref)
    left, right = exponent_sides(query_ref[...], train_ref[...])
    left_ref[...] = left.T
    right_ref[...] = right
    w_copy.start()

    def cross(tb):
        rows = slice(tb * 256, tb * 256 + 256)
        kernel = jnp.exp(jnp.dot(left_ref[rows, :], right_ref[...], preferred_element_type=F32))
        high = kernel.astype(BF16)
        kh[rows, :] = high
        kl[rows, :] = (kernel - high.astype(F32)).astype(BF16)

    def explain(tb):
        rows = slice(tb * 256, tb * 256 + 256)
        squares = jnp.zeros((256, 128), F32)
        for b in range(4):
            block = slice(b * 256, b * 256 + 256), slice(0, 256 * (b + 1))
            whitened = dot_nt(kh[rows, block[1]], lb[block])
            whitened += dot_nt(kl[rows, block[1]], lb[block])
            whitened += dot_nt(kh[rows, block[1]], ll[block])
            squares += whitened[:, :128] * whitened[:, :128] + whitened[:, 128:] * whitened[:, 128:]
        explained = jnp.sum(squares, axis=1, keepdims=True)
        post_var = PRIOR_VAR - explained
        beta = 0.5 * (jnp.log(jnp.full_like(post_var, PRIOR_VAR)) - jnp.log(post_var))
        term = beta / post_var
        term_ref[rows, :] = term
        q = term - beta / PRIOR_VAR
        for i in range(2):
            lanes = jnp.sum(jnp.where(eye, q[i * 128 : i * 128 + 128], 0.0), axis=0, keepdims=True)
            q_ref[tb * 2 + i : tb * 2 + i + 1, :] = lanes

    eye = lax.broadcasted_iota(jnp.int32, (128, 128), 0) == lax.broadcasted_iota(jnp.int32, (128, 128), 1)
    for tb in range(NK):
        cross(tb)
    for copy in l_copies:
        copy.wait()
    for b in range(4):
        block = slice(b * 256, b * 256 + 256), slice(0, 256 * (b + 1))
        factor = lf[block]
        high = factor.astype(BF16)
        lb[block] = high
        ll[block] = (factor - high.astype(F32)).astype(BF16)
    for tb in range(4):
        if tb + NK < 4:
            cross(tb + NK)
        explain(tb)

    w_copy.wait()
    b_copy.start()
    m_copy.start()
    wb[...] = wf[...].astype(BF16)

    q = q_ref[...]
    core_copies = []
    for g in range(4):
        rows = slice(g * 256, g * 256 + 256)
        mean = jnp.dot(kh[rows, :], wb[...], preferred_element_type=F32) * term_ref[rows, :]
        c_send[g, :, :32] = tiles(mean).reshape(2, 32, 16, 128)
        n = 32
        if g == 0:
            n = 33
            c_send[0, :, 32] = jnp.broadcast_to(jnp.concatenate([q, q], 0)[None], (2, 16, 128))
            pl.semaphore_wait(barrier, len(everyone))
        core_copies.append(send(c_send.at[g, 1 - core, pl.ds(0, n)], c_recv.at[g, pl.ds(0, n)], c_s.at[g], c_r.at[g], partner))

    for g in range(4):
        core_copies[g].wait()
        mine = (c_send[g, core, :32] + c_recv[g, :32]).reshape(16, 2, 16, 128)
        own[g] = mine
        if g == 0:
            p_send0[:, :2] = mine.astype(BF16)
            q += c_recv[0, 32, :8]
            p_send0[:, 2] = jnp.broadcast_to(split_q(q)[None], (16, 16, 128))
        else:
            p_send[g - 1] = mine.astype(BF16)
        for k, (dx, dy) in enumerate(PLANE):
            to = ((x + dx) % 4) * 4 + (y + dy) % 4
            src, dst = (p_send0.at[to], p_recv0.at[k]) if g == 0 else (p_send.at[g - 1, to], p_recv.at[g - 1, k])
            send(src, dst, p_s.at[g], p_r.at[g], plane_peers[k])

    for g in range(4):
        total = own[g, plane]
        wait_all(p_recv0 if g == 0 else p_recv.at[g - 1], p_s.at[g], p_r.at[g], plane_peers[0])
        for k in range(15):
            if g == 0:
                total += p_recv0[k, :2].astype(F32)
                q += join_q(p_recv0[k, 2])
            else:
                total += p_recv[g - 1, k].astype(F32)
        z_own[g] = total
        z_send[g, :2] = total.astype(BF16)
        if g == 0:
            z_send[0, 2] = split_q(q)
        for k in range(7):
            src, dst = (z_send.at[0], z_recv0.at[k]) if g == 0 else (z_send.at[g, pl.ds(0, 2)], z_recv.at[g - 1, k])
            send(src, dst, z_s.at[g], z_r.at[g], z_peers[k])

    b_copy.wait()
    m_copy.wait()
    row = lax.broadcasted_iota(jnp.int32, (8, 128), 0)
    pick_row = lax.broadcasted_iota(jnp.int32, (16, 128), 0) + (plane // 2) * 16
    pick = lax.broadcasted_iota(jnp.int32, (16, 128), 1) == pick_row
    for g in range(4):
        total = z_own[g]
        wait_all(z_recv0 if g == 0 else z_recv.at[g - 1], z_s.at[g], z_r.at[g], z_peers[0])
        for k in range(7):
            if g == 0:
                total += z_recv0[k, :2].astype(F32)
                q += join_q(z_recv0[k, 2])
            else:
                total += z_recv[g - 1, k].astype(F32)
        if g == 0:
            precision = q + 1.0 / PRIOR_VAR
        line = jnp.sum(jnp.where(row == g * 2 + core, precision, 0.0), axis=0, keepdims=True)
        column = jnp.sum(jnp.where(pick, line, 0.0), axis=1, keepdims=True)
        spot = coef.at[(g * 2 + core) * 8 + plane // 2, pl.ds((plane % 2) * 2, 2)]
        coef[(g * 2 + core) * 8 + plane // 2, pl.ds((plane % 2) * 2, 2)] = (total / column).astype(BF16)
        for k in range(15):
            send(spot, spot, g_s.at[g], g_r.at[g], plane_peers[k])

    def field(g):
        c = rows_of(coef[g * 16 : g * 16 + 16])
        out_ref[g * 256 : g * 256 + 256, :] = (jnp.dot(c, basis_v[...], preferred_element_type=F32) + clim_ref[...]).astype(BF16)

    last = []
    for g in range(4):
        wait_all(p_recv.at[0], g_s.at[g], g_r.at[g], plane_peers[0])
        half = coef.at[pl.ds((g * 2 + core) * 8, 8)]
        last.append(send(half, half, h_s.at[g], h_r.at[g], partner))
    for g in range(3):
        last[g].wait()
    for g in range(3):
        field(g)
    last[3].wait()
    field(3)


VM = pl.BlockSpec(memory_space=pltpu.VMEM)
HBM = pl.BlockSpec(memory_space=pltpu.HBM)


def body(train_inputs, inv_factor, weights, candidates, test_ids, basis, climatology):
    arrays = train_inputs[0], candidates, test_ids.reshape(8, 128), inv_factor[0], weights[0], basis, climatology.reshape(1, 1024)
    dma = pltpu.SemaphoreType.DMA
    tile = lambda *n: pltpu.VMEM((*n, 16, 128), BF16)
    tile32 = lambda *n: pltpu.VMEM((*n, 16, 128), F32)
    return pl.pallas_call(
        main_kernel,
        out_shape=jax.ShapeDtypeStruct((1024, 1024), BF16),
        in_specs=[HBM] * 7,
        out_specs=VM,
        scratch_shapes=[
            pltpu.VMEM((16, 1024), F32), pltpu.VMEM((16, 4096), F32), pltpu.VMEM((8, 128), jnp.int32), pltpu.VMEM((16, 1024), F32),
            pltpu.VMEM((1024, 128), BF16), pltpu.VMEM((128, 1024), BF16),
            pltpu.VMEM((1024, 1024), F32), pltpu.VMEM((1024, 1024), BF16), pltpu.VMEM((1024, 1024), BF16),
            pltpu.VMEM((1024, 512), F32), pltpu.VMEM((1024, 512), BF16), pltpu.VMEM((512, 1024), BF16), pltpu.VMEM((1, 1024), F32),
            pltpu.VMEM((1024, 1024), BF16), pltpu.VMEM((1024, 1024), BF16),
            pltpu.VMEM((1024, 1), F32), pltpu.VMEM((8, 128), F32),
            tile32(4, 2, 33), tile32(4, 33), tile32(4, 16, 2),
            tile(16, 3), tile(3, 16, 2), tile(15, 3), tile(3, 15, 2), tile(4, 3), tile(7, 3), tile(3, 7, 2), tile32(4, 2), tile(64, 4),
            dma((3,)), dma((4,)), dma, dma, dma, dma((4,)), dma((4,)), *[dma((4,))] * 8,
        ],
        compiler_params=pltpu.CompilerParams(collective_id=0, has_side_effects=True, vmem_limit_bytes=44 << 20),
    )(*[pltpu.with_memory_space_constraint(a, pltpu.HBM) for a in arrays])


def solution(mesh):
    both = ("group", "expert")
    return jax.shard_map(
        body,
        mesh=mesh,
        in_specs=(P(both, None, None), P(both, None, None), P(both, None, None), P(), P(), P(None, both), P(both)),
        out_specs=P(None, both),
        check_vma=False,
    )
```

```python
import functools

import jax
import jax.numpy as jnp
from jax import lax
from jax.experimental import pallas as pl
from jax.experimental.pallas import tpu as pltpu
from jax.sharding import PartitionSpec as P

MESH = pl.DeviceIdType.MESH
F32, BF16, F8 = jnp.float32, jnp.bfloat16, jnp.float8_e4m3fn
PRIOR_VAR = 1.1
NK = 2
PLANE = [(dx, dy) for dx in range(4) for dy in range(4) if dx or dy]
PLANE.sort(key=lambda d: -(min(d[0], 4 - d[0]) + min(d[1], 4 - d[1])))
ALONG = [4, 3, 5, 2, 6, 1, 7]


def split3(a):
    hi = a.astype(BF16)
    rest = a - hi.astype(F32)
    mid = rest.astype(BF16)
    low = (rest - mid.astype(F32)).astype(BF16)
    return hi, mid, low


def gather_queries(cand_ref, ids_ref, query_ref):
    for tb in range(8):
        ids = jnp.broadcast_to(ids_ref[tb : tb + 1, :], (8, 128))
        lane, block = ids & 127, ids >> 7
        for half in range(2):
            rows = slice(half * 8, half * 8 + 8)
            got = jnp.zeros((8, 128), F32)
            for h in range(32):
                values = jnp.take_along_axis(
                    cand_ref[rows, h * 128 : h * 128 + 128], lane, axis=1, mode="promise_in_bounds"
                )
                got = jnp.where(block == h, values, got)
            query_ref[rows, tb * 128 : tb * 128 + 128] = got


def exponent_sides(query, train):
    qh, qm, ql = split3(query)
    xh, xm, xl = split3(train)
    t = split3(-0.5 * jnp.sum(query * query, axis=0, keepdims=True))
    s = split3(-0.5 * jnp.sum(train * train, axis=0, keepdims=True))
    row = lax.broadcasted_iota(jnp.int32, query.shape, 0)

    def rows(first, parts):
        out = jnp.zeros(query.shape, F32)
        for i, part in enumerate(parts):
            out = jnp.where(row == first + i, part.astype(F32), out)
        return out

    ones = lambda first: jnp.where((row >= first) & (row < first + 3), 1.0, 0.0)
    zero = jnp.zeros(query.shape, BF16)
    left = [qh, qh, qm, qm, qh, ql, (rows(0, t) + ones(3)).astype(BF16), zero]
    right = [xh, xm, xh, xm, xl, xh, (rows(3, s) + ones(0)).astype(BF16), zero]
    return jnp.concatenate(left, 0), jnp.concatenate(right, 0)


def dot_nt(a, b):
    return lax.dot_general(a, b, (((1,), (1,)), ((), ())), preferred_element_type=F32)


def place():
    group, expert = lax.axis_index("group"), lax.axis_index("expert")
    return group // 8, group % 8, expert // 4, (expert // 2) % 2, expert % 2


def device(x, y, z, core):
    return ((y % 2) * 8 + z, x * 4 + (y // 2) * 2 + core)


def split_q(q):
    hi = q.astype(BF16).astype(F32)
    return jnp.concatenate([hi, q - hi], 0).astype(BF16)


def join_q(tile):
    tile = tile.astype(F32)
    return tile[:8] + tile[8:]


def tiles(a):
    return jnp.stack([a[:, cb * 128 : cb * 128 + 128].reshape(-1, 16, 128) for cb in range(4)], axis=1)


def rows_of(t):
    return jnp.concatenate([t[:, cb].reshape(-1, 128) for cb in range(4)], axis=1)


def main_kernel(train_hbm, cand_hbm, ids_hbm, factor_ref, weights_ref, basis_ref, clim_hbm, out_ref,
                train_ref, cand_ref, ids_ref, query_ref, left_ref, right_ref, lf, lb, l8, wf, wb, basis_v, clim_ref, kh, k8, term_ref, q_ref,
                c_send, c_recv, own, p_send0, p_send, p_recv0, p_recv, z_send, z_recv0, z_recv, z_own, coef,
                i_sem, l_sem, w_sem, b_sem, m_sem, c_s, c_r, p_s, p_r, z_s, z_r, g_s, g_r, h_s, h_r):
    y_lo, z, x, y_hi, core = place()
    y = y_hi * 2 + y_lo
    plane = x * 4 + y
    partner = device(x, y, z, 1 - core)
    plane_peers = [device((x + dx) % 4, (y + dy) % 4, z, core) for dx, dy in PLANE]
    z_peers = [device(x, y, (z + d) % 8, core) for d in ALONG]

    copies = [
        pltpu.make_async_copy(ids_hbm, ids_ref, i_sem.at[0]),
        pltpu.make_async_copy(cand_hbm, cand_ref, i_sem.at[1]),
        pltpu.make_async_copy(train_hbm, train_ref, i_sem.at[2]),
    ]
    for copy in copies:
        copy.start()
    l_copies = []
    for b in range(4):
        block = pl.ds(b * 256, 256), pl.ds(0, 256 * (b + 1))
        l_copies.append(pltpu.make_async_copy(factor_ref.at[block], lf.at[block], l_sem.at[b]))
    w_copy = pltpu.make_async_copy(weights_ref, wf, w_sem)
    m_copy = pltpu.make_async_copy(clim_hbm, clim_ref, m_sem)
    b_copy = pltpu.make_async_copy(basis_ref, basis_v, b_sem)
    for copy in l_copies:
        copy.start()

    barrier = pltpu.get_barrier_semaphore()
    everyone = [partner] + plane_peers + z_peers
    for peer in everyone:
        pl.semaphore_signal(barrier, inc=1, device_id=peer, device_id_type=MESH)

    def send(src, dst, s_sem, r_sem, peer):
        copy = pltpu.make_async_remote_copy(
            src_ref=src, dst_ref=dst, send_sem=s_sem, recv_sem=r_sem, device_id=peer, device_id_type=MESH
        )
        copy.start()
        return copy

    def wait_all(like, s_sem, r_sem, peer):
        pltpu.make_async_remote_copy(
            src_ref=like, dst_ref=like, send_sem=s_sem, recv_sem=r_sem, device_id=peer, device_id_type=MESH
        ).wait()

    for copy in copies:
        copy.wait()
    gather_queries(cand_ref, ids_ref, query_ref)
    left, right = exponent_sides(query_ref[...], train_ref[...])
    left_ref[...] = left.T
    right_ref[...] = right
    w_copy.start()

    def cross(tb):
        rows = slice(tb * 256, tb * 256 + 256)
        kernel = jnp.exp(jnp.dot(left_ref[rows, :], right_ref[...], preferred_element_type=F32))
        high = kernel.astype(BF16)
        kh[rows, :] = high
        low = ((kernel - high.astype(F32)) * 4096.0).astype(F8)
        top = (kernel * 16.0).astype(F8)
        for i in range(4):
            k8[rows, i * 512 : i * 512 + 256] = low[:, i * 256 : i * 256 + 256]
            k8[rows, i * 512 + 256 : i * 512 + 512] = top[:, i * 256 : i * 256 + 256]

    def explain(tb):
        rows = slice(tb * 256, tb * 256 + 256)
        squares = jnp.zeros((256, 128), F32)
        for b in range(4):
            block = slice(b * 256, b * 256 + 256), slice(0, 256 * (b + 1))
            whitened = dot_nt(kh[rows, block[1]], lb[block])
            whitened += dot_nt(k8[rows, : 512 * (b + 1)], l8[block[0], : 512 * (b + 1)]) * 2.0**-15
            squares += whitened[:, :128] * whitened[:, :128] + whitened[:, 128:] * whitened[:, 128:]
        explained = jnp.sum(squares, axis=1, keepdims=True)
        post_var = PRIOR_VAR - explained
        beta = 0.5 * (jnp.log(jnp.full_like(post_var, PRIOR_VAR)) - jnp.log(post_var))
        term = beta / post_var
        term_ref[rows, :] = term
        q = term - beta / PRIOR_VAR
        for i in range(2):
            lanes = jnp.sum(jnp.where(eye, q[i * 128 : i * 128 + 128], 0.0), axis=0, keepdims=True)
            q_ref[tb * 2 + i : tb * 2 + i + 1, :] = lanes

    eye = lax.broadcasted_iota(jnp.int32, (128, 128), 0) == lax.broadcasted_iota(jnp.int32, (128, 128), 1)
    for tb in range(NK):
        cross(tb)
    for copy in l_copies:
        copy.wait()
    for b in range(4):
        block = slice(b * 256, b * 256 + 256), slice(0, 256 * (b + 1))
        factor = lf[block]
        high = factor.astype(BF16)
        lb[block] = high
        low = ((factor - high.astype(F32)) * 2048.0).astype(F8)
        top = (factor * 8.0).astype(F8)
        for i in range(b + 1):
            l8[block[0], i * 512 : i * 512 + 256] = top[:, i * 256 : i * 256 + 256]
            l8[block[0], i * 512 + 256 : i * 512 + 512] = low[:, i * 256 : i * 256 + 256]
    for tb in range(4):
        if tb + NK < 4:
            cross(tb + NK)
        explain(tb)

    w_copy.wait()
    b_copy.start()
    m_copy.start()
    wb[...] = wf[...].astype(BF16)

    q = q_ref[...]
    core_copies = []
    for g in range(4):
        rows = slice(g * 256, g * 256 + 256)
        mean = jnp.dot(kh[rows, :], wb[...], preferred_element_type=F32) * term_ref[rows, :]
        c_send[g, :, :32] = tiles(mean).reshape(2, 32, 16, 128)
        n = 32
        if g == 0:
            n = 33
            c_send[0, :, 32] = jnp.broadcast_to(jnp.concatenate([q, q], 0)[None], (2, 16, 128))
            pl.semaphore_wait(barrier, len(everyone))
        core_copies.append(send(c_send.at[g, 1 - core, pl.ds(0, n)], c_recv.at[g, pl.ds(0, n)], c_s.at[g], c_r.at[g], partner))

    for g in range(4):
        core_copies[g].wait()
        mine = (c_send[g, core, :32] + c_recv[g, :32]).reshape(16, 2, 16, 128)
        own[g] = mine
        if g == 0:
            p_send0[:, :2] = mine.astype(BF16)
            q += c_recv[0, 32, :8]
            p_send0[:, 2] = jnp.broadcast_to(split_q(q)[None], (16, 16, 128))
        else:
            p_send[g - 1] = mine.astype(BF16)
        for k, (dx, dy) in enumerate(PLANE):
            to = ((x + dx) % 4) * 4 + (y + dy) % 4
            src, dst = (p_send0.at[to], p_recv0.at[k]) if g == 0 else (p_send.at[g - 1, to], p_recv.at[g - 1, k])
            send(src, dst, p_s.at[g], p_r.at[g], plane_peers[k])

    for g in range(4):
        total = own[g, plane]
        wait_all(p_recv0 if g == 0 else p_recv.at[g - 1], p_s.at[g], p_r.at[g], plane_peers[0])
        for k in range(15):
            if g == 0:
                total += p_recv0[k, :2].astype(F32)
                q += join_q(p_recv0[k, 2])
            else:
                total += p_recv[g - 1, k].astype(F32)
        z_own[g] = total
        z_send[g, :2] = total.astype(BF16)
        if g == 0:
            z_send[0, 2] = split_q(q)
        for k in range(7):
            src, dst = (z_send.at[0], z_recv0.at[k]) if g == 0 else (z_send.at[g, pl.ds(0, 2)], z_recv.at[g - 1, k])
            send(src, dst, z_s.at[g], z_r.at[g], z_peers[k])

    b_copy.wait()
    m_copy.wait()
    row = lax.broadcasted_iota(jnp.int32, (8, 128), 0)
    pick_row = lax.broadcasted_iota(jnp.int32, (16, 128), 0) + (plane // 2) * 16
    pick = lax.broadcasted_iota(jnp.int32, (16, 128), 1) == pick_row
    for g in range(4):
        total = z_own[g]
        wait_all(z_recv0 if g == 0 else z_recv.at[g - 1], z_s.at[g], z_r.at[g], z_peers[0])
        for k in range(7):
            if g == 0:
                total += z_recv0[k, :2].astype(F32)
                q += join_q(z_recv0[k, 2])
            else:
                total += z_recv[g - 1, k].astype(F32)
        if g == 0:
            precision = q + 1.0 / PRIOR_VAR
        line = jnp.sum(jnp.where(row == g * 2 + core, precision, 0.0), axis=0, keepdims=True)
        column = jnp.sum(jnp.where(pick, line, 0.0), axis=1, keepdims=True)
        spot = coef.at[(g * 2 + core) * 8 + plane // 2, pl.ds((plane % 2) * 2, 2)]
        coef[(g * 2 + core) * 8 + plane // 2, pl.ds((plane % 2) * 2, 2)] = (total / column).astype(BF16)
        for k in range(15):
            send(spot, spot, g_s.at[g], g_r.at[g], plane_peers[k])

    def field(g):
        c = rows_of(coef[g * 16 : g * 16 + 16])
        out_ref[g * 256 : g * 256 + 256, :] = (jnp.dot(c, basis_v[...], preferred_element_type=F32) + clim_ref[...]).astype(BF16)

    last = []
    for g in range(4):
        wait_all(p_recv.at[0], g_s.at[g], g_r.at[g], plane_peers[0])
        half = coef.at[pl.ds((g * 2 + core) * 8, 8)]
        last.append(send(half, half, h_s.at[g], h_r.at[g], partner))
    for g in range(3):
        last[g].wait()
    for g in range(3):
        field(g)
    last[3].wait()
    field(3)


VM = pl.BlockSpec(memory_space=pltpu.VMEM)
HBM = pl.BlockSpec(memory_space=pltpu.HBM)


def body(train_inputs, inv_factor, weights, candidates, test_ids, basis, climatology):
    arrays = train_inputs[0], candidates, test_ids.reshape(8, 128), inv_factor[0], weights[0], basis, climatology.reshape(1, 1024)
    dma = pltpu.SemaphoreType.DMA
    tile = lambda *n: pltpu.VMEM((*n, 16, 128), BF16)
    tile32 = lambda *n: pltpu.VMEM((*n, 16, 128), F32)
    return pl.pallas_call(
        main_kernel,
        out_shape=jax.ShapeDtypeStruct((1024, 1024), BF16),
        in_specs=[HBM] * 7,
        out_specs=VM,
        scratch_shapes=[
            pltpu.VMEM((16, 1024), F32), pltpu.VMEM((16, 4096), F32), pltpu.VMEM((8, 128), jnp.int32), pltpu.VMEM((16, 1024), F32),
            pltpu.VMEM((1024, 128), BF16), pltpu.VMEM((128, 1024), BF16),
            pltpu.VMEM((1024, 1024), F32), pltpu.VMEM((1024, 1024), BF16), pltpu.VMEM((1024, 2048), F8),
            pltpu.VMEM((1024, 512), F32), pltpu.VMEM((1024, 512), BF16), pltpu.VMEM((512, 1024), BF16), pltpu.VMEM((1, 1024), F32),
            pltpu.VMEM((1024, 1024), BF16), pltpu.VMEM((1024, 2048), F8),
            pltpu.VMEM((1024, 1), F32), pltpu.VMEM((8, 128), F32),
            tile32(4, 2, 33), tile32(4, 33), tile32(4, 16, 2),
            tile(16, 3), tile(3, 16, 2), tile(15, 3), tile(3, 15, 2), tile(4, 3), tile(7, 3), tile(3, 7, 2), tile32(4, 2), tile(64, 4),
            dma((3,)), dma((4,)), dma, dma, dma, dma((4,)), dma((4,)), *[dma((4,))] * 8,
        ],
        compiler_params=pltpu.CompilerParams(collective_id=0, has_side_effects=True, vmem_limit_bytes=44 << 20),
    )(*[pltpu.with_memory_space_constraint(a, pltpu.HBM) for a in arrays])


def solution(mesh):
    both = ("group", "expert")
    return jax.shard_map(
        body,
        mesh=mesh,
        in_specs=(P(both, None, None), P(both, None, None), P(both, None, None), P(), P(), P(None, both), P(both)),
        out_specs=P(None, both),
        check_vma=False,
    )
```

```python
import functools

import jax
import jax.numpy as jnp
from jax import lax
from jax.experimental import pallas as pl
from jax.experimental.pallas import tpu as pltpu
from jax.sharding import PartitionSpec as P

MESH = pl.DeviceIdType.MESH
F32, BF16, F8 = jnp.float32, jnp.bfloat16, jnp.float8_e4m3fn
PRIOR_VAR = 1.1
NK = 2
PLANE = [(dx, dy) for dx in range(4) for dy in range(4) if dx or dy]
PLANE.sort(key=lambda d: -(min(d[0], 4 - d[0]) + min(d[1], 4 - d[1])))
ALONG = [4, 3, 5, 2, 6, 1, 7]


def split3(a):
    hi = a.astype(BF16)
    rest = a - hi.astype(F32)
    mid = rest.astype(BF16)
    low = (rest - mid.astype(F32)).astype(BF16)
    return hi, mid, low


def gather_queries(cand_ref, ids_ref, query_ref):
    for tb in range(8):
        ids = jnp.broadcast_to(ids_ref[tb : tb + 1, :], (8, 128))
        lane, block = ids & 127, ids >> 7
        for half in range(2):
            rows = slice(half * 8, half * 8 + 8)
            got = jnp.zeros((8, 128), F32)
            for h in range(32):
                values = jnp.take_along_axis(
                    cand_ref[rows, h * 128 : h * 128 + 128], lane, axis=1, mode="promise_in_bounds"
                )
                got = jnp.where(block == h, values, got)
            query_ref[rows, tb * 128 : tb * 128 + 128] = got


def exponent_sides(query, train):
    qh, qm, ql = split3(query)
    xh, xm, xl = split3(train)
    t = split3(-0.5 * jnp.sum(query * query, axis=0, keepdims=True))
    s = split3(-0.5 * jnp.sum(train * train, axis=0, keepdims=True))
    row = lax.broadcasted_iota(jnp.int32, query.shape, 0)

    def rows(first, parts):
        out = jnp.zeros(query.shape, F32)
        for i, part in enumerate(parts):
            out = jnp.where(row == first + i, part.astype(F32), out)
        return out

    ones = lambda first: jnp.where((row >= first) & (row < first + 3), 1.0, 0.0)
    zero = jnp.zeros(query.shape, BF16)
    left = [qh, qh, qm, qm, qh, ql, (rows(0, t) + ones(3)).astype(BF16), zero]
    right = [xh, xm, xh, xm, xl, xh, (rows(3, s) + ones(0)).astype(BF16), zero]
    return jnp.concatenate(left, 0), jnp.concatenate(right, 0)


def dot_nt(a, b):
    return lax.dot_general(a, b, (((1,), (1,)), ((), ())), preferred_element_type=F32)


def place():
    group, expert = lax.axis_index("group"), lax.axis_index("expert")
    return group // 8, group % 8, expert // 4, (expert // 2) % 2, expert % 2


def device(x, y, z, core):
    return ((y % 2) * 8 + z, x * 4 + (y // 2) * 2 + core)


def split_q(q):
    hi = q.astype(BF16).astype(F32)
    return jnp.concatenate([hi, q - hi], 0).astype(BF16)


def join_q(tile):
    tile = tile.astype(F32)
    return tile[:8] + tile[8:]


def tiles(a):
    return jnp.stack([a[:, cb * 128 : cb * 128 + 128].reshape(-1, 16, 128) for cb in range(4)], axis=1)


def rows_of(t):
    return jnp.concatenate([t[:, cb].reshape(-1, 128) for cb in range(4)], axis=1)


def main_kernel(train_hbm, cand_hbm, ids_hbm, factor_ref, weights_ref, basis_ref, clim_hbm, out_ref,
                train_ref, cand_ref, ids_ref, query_ref, left_ref, right_ref, lf, lb, l8, wf, wb, basis_v, clim_ref, kh, k8, term_ref, q_ref,
                c_send, c_recv, own, p_send0, p_send, p_recv0, p_recv, z_send, z_recv0, z_recv, z_own, coef,
                i_sem, l_sem, w_sem, b_sem, m_sem, c_s, c_r, p_s, p_r, z_s, z_r, g_s, g_r, h_s, h_r):
    y_lo, z, x, y_hi, core = place()
    y = y_hi * 2 + y_lo
    plane = x * 4 + y
    partner = device(x, y, z, 1 - core)
    plane_peers = [device((x + dx) % 4, (y + dy) % 4, z, core) for dx, dy in PLANE]
    z_peers = [device(x, y, (z + d) % 8, core) for d in ALONG]

    copies = [
        pltpu.make_async_copy(ids_hbm, ids_ref, i_sem.at[0]),
        pltpu.make_async_copy(cand_hbm, cand_ref, i_sem.at[1]),
        pltpu.make_async_copy(train_hbm, train_ref, i_sem.at[2]),
    ]
    for copy in copies:
        copy.start()
    l_copies = []
    for b in range(4):
        block = pl.ds(b * 256, 256), pl.ds(0, 256 * (b + 1))
        l_copies.append(pltpu.make_async_copy(factor_ref.at[block], lf.at[block], l_sem.at[b]))
    w_copy = pltpu.make_async_copy(weights_ref, wf, w_sem)
    m_copy = pltpu.make_async_copy(clim_hbm, clim_ref, m_sem)
    b_copy = pltpu.make_async_copy(basis_ref, basis_v, b_sem)
    for copy in l_copies:
        copy.start()

    barrier = pltpu.get_barrier_semaphore()
    everyone = [partner] + plane_peers + z_peers
    for peer in everyone:
        pl.semaphore_signal(barrier, inc=1, device_id=peer, device_id_type=MESH)

    def send(src, dst, s_sem, r_sem, peer):
        copy = pltpu.make_async_remote_copy(
            src_ref=src, dst_ref=dst, send_sem=s_sem, recv_sem=r_sem, device_id=peer, device_id_type=MESH
        )
        copy.start()
        return copy

    sent = []

    def wait_all(like, s_sem, r_sem, peer):
        copy = pltpu.make_async_remote_copy(
            src_ref=like, dst_ref=like, send_sem=s_sem, recv_sem=r_sem, device_id=peer, device_id_type=MESH
        )
        copy.wait_recv()
        sent.append(copy)

    for copy in copies:
        copy.wait()
    gather_queries(cand_ref, ids_ref, query_ref)
    left, right = exponent_sides(query_ref[...], train_ref[...])
    left_ref[...] = left.T
    right_ref[...] = right
    w_copy.start()

    def cross(tb):
        rows = slice(tb * 256, tb * 256 + 256)
        kernel = jnp.exp(jnp.dot(left_ref[rows, :], right_ref[...], preferred_element_type=F32))
        high = kernel.astype(BF16)
        kh[rows, :] = high
        low = ((kernel - high.astype(F32)) * 4096.0).astype(F8)
        top = (kernel * 16.0).astype(F8)
        for i in range(4):
            k8[rows, i * 512 : i * 512 + 256] = low[:, i * 256 : i * 256 + 256]
            k8[rows, i * 512 + 256 : i * 512 + 512] = top[:, i * 256 : i * 256 + 256]

    def explain(tb):
        rows = slice(tb * 256, tb * 256 + 256)
        squares = jnp.zeros((256, 128), F32)
        for b in range(4):
            block = slice(b * 256, b * 256 + 256), slice(0, 256 * (b + 1))
            whitened = dot_nt(kh[rows, block[1]], lb[block])
            whitened += dot_nt(k8[rows, : 512 * (b + 1)], l8[block[0], : 512 * (b + 1)]) * 2.0**-15
            squares += whitened[:, :128] * whitened[:, :128] + whitened[:, 128:] * whitened[:, 128:]
        explained = jnp.sum(squares, axis=1, keepdims=True)
        post_var = PRIOR_VAR - explained
        beta = 0.5 * (jnp.log(jnp.full_like(post_var, PRIOR_VAR)) - jnp.log(post_var))
        term = beta / post_var
        term_ref[rows, :] = term
        q = term - beta / PRIOR_VAR
        for i in range(2):
            lanes = jnp.sum(jnp.where(eye, q[i * 128 : i * 128 + 128], 0.0), axis=0, keepdims=True)
            q_ref[tb * 2 + i : tb * 2 + i + 1, :] = lanes

    eye = lax.broadcasted_iota(jnp.int32, (128, 128), 0) == lax.broadcasted_iota(jnp.int32, (128, 128), 1)
    for tb in range(NK):
        cross(tb)
    for copy in l_copies:
        copy.wait()
    for b in range(4):
        block = slice(b * 256, b * 256 + 256), slice(0, 256 * (b + 1))
        factor = lf[block]
        high = factor.astype(BF16)
        lb[block] = high
        low = ((factor - high.astype(F32)) * 2048.0).astype(F8)
        top = (factor * 8.0).astype(F8)
        for i in range(b + 1):
            l8[block[0], i * 512 : i * 512 + 256] = top[:, i * 256 : i * 256 + 256]
            l8[block[0], i * 512 + 256 : i * 512 + 512] = low[:, i * 256 : i * 256 + 256]
    for tb in range(4):
        if tb + NK < 4:
            cross(tb + NK)
        explain(tb)

    w_copy.wait()
    b_copy.start()
    m_copy.start()
    wb[...] = wf[...].astype(BF16)

    q = q_ref[...]
    core_copies = []
    for g in range(4):
        rows = slice(g * 256, g * 256 + 256)
        mean = jnp.dot(kh[rows, :], wb[...], preferred_element_type=F32) * term_ref[rows, :]
        c_send[g, :, :32] = tiles(mean).reshape(2, 32, 16, 128)
        n = 32
        if g == 0:
            n = 33
            c_send[0, :, 32] = jnp.broadcast_to(jnp.concatenate([q, q], 0)[None], (2, 16, 128))
            pl.semaphore_wait(barrier, len(everyone))
        core_copies.append(send(c_send.at[g, 1 - core, pl.ds(0, n)], c_recv.at[g, pl.ds(0, n)], c_s.at[g], c_r.at[g], partner))

    for g in range(4):
        core_copies[g].wait_recv()
        sent.append(core_copies[g])
        mine = (c_send[g, core, :32] + c_recv[g, :32]).reshape(16, 2, 16, 128)
        own[g] = mine
        if g == 0:
            p_send0[:, :2] = mine.astype(BF16)
            q += c_recv[0, 32, :8]
            p_send0[:, 2] = jnp.broadcast_to(split_q(q)[None], (16, 16, 128))
        else:
            p_send[g - 1] = mine.astype(BF16)
        for k, (dx, dy) in enumerate(PLANE):
            to = ((x + dx) % 4) * 4 + (y + dy) % 4
            src, dst = (p_send0.at[to], p_recv0.at[k]) if g == 0 else (p_send.at[g - 1, to], p_recv.at[g - 1, k])
            send(src, dst, p_s.at[g], p_r.at[g], plane_peers[k])

    for g in range(4):
        total = own[g, plane]
        wait_all(p_recv0 if g == 0 else p_recv.at[g - 1], p_s.at[g], p_r.at[g], plane_peers[0])
        for k in range(15):
            if g == 0:
                total += p_recv0[k, :2].astype(F32)
                q += join_q(p_recv0[k, 2])
            else:
                total += p_recv[g - 1, k].astype(F32)
        z_own[g] = total
        z_send[g, :2] = total.astype(BF16)
        if g == 0:
            z_send[0, 2] = split_q(q)
        for k in range(7):
            src, dst = (z_send.at[0], z_recv0.at[k]) if g == 0 else (z_send.at[g, pl.ds(0, 2)], z_recv.at[g - 1, k])
            send(src, dst, z_s.at[g], z_r.at[g], z_peers[k])

    b_copy.wait()
    m_copy.wait()
    row = lax.broadcasted_iota(jnp.int32, (8, 128), 0)
    pick_row = lax.broadcasted_iota(jnp.int32, (16, 128), 0) + (plane // 2) * 16
    pick = lax.broadcasted_iota(jnp.int32, (16, 128), 1) == pick_row
    for g in range(4):
        total = z_own[g]
        wait_all(z_recv0 if g == 0 else z_recv.at[g - 1], z_s.at[g], z_r.at[g], z_peers[0])
        for k in range(7):
            if g == 0:
                total += z_recv0[k, :2].astype(F32)
                q += join_q(z_recv0[k, 2])
            else:
                total += z_recv[g - 1, k].astype(F32)
        if g == 0:
            precision = q + 1.0 / PRIOR_VAR
        line = jnp.sum(jnp.where(row == g * 2 + core, precision, 0.0), axis=0, keepdims=True)
        column = jnp.sum(jnp.where(pick, line, 0.0), axis=1, keepdims=True)
        spot = coef.at[(g * 2 + core) * 8 + plane // 2, pl.ds((plane % 2) * 2, 2)]
        coef[(g * 2 + core) * 8 + plane // 2, pl.ds((plane % 2) * 2, 2)] = (total / column).astype(BF16)
        for k in range(15):
            send(spot, spot, g_s.at[g], g_r.at[g], plane_peers[k])

    def field(g):
        c = rows_of(coef[g * 16 : g * 16 + 16])
        out_ref[g * 256 : g * 256 + 256, :] = (jnp.dot(c, basis_v[...], preferred_element_type=F32) + clim_ref[...]).astype(BF16)

    last = []
    for g in range(4):
        wait_all(p_recv.at[0], g_s.at[g], g_r.at[g], plane_peers[0])
        half = coef.at[pl.ds((g * 2 + core) * 8, 8)]
        last.append(send(half, half, h_s.at[g], h_r.at[g], partner))
    for g in range(3):
        last[g].wait()
    for g in range(3):
        field(g)
    last[3].wait()
    field(3)
    for copy in sent:
        copy.wait_send()


VM = pl.BlockSpec(memory_space=pltpu.VMEM)
HBM = pl.BlockSpec(memory_space=pltpu.HBM)


def body(train_inputs, inv_factor, weights, candidates, test_ids, basis, climatology):
    arrays = train_inputs[0], candidates, test_ids.reshape(8, 128), inv_factor[0], weights[0], basis, climatology.reshape(1, 1024)
    dma = pltpu.SemaphoreType.DMA
    tile = lambda *n: pltpu.VMEM((*n, 16, 128), BF16)
    tile32 = lambda *n: pltpu.VMEM((*n, 16, 128), F32)
    return pl.pallas_call(
        main_kernel,
        out_shape=jax.ShapeDtypeStruct((1024, 1024), BF16),
        in_specs=[HBM] * 7,
        out_specs=VM,
        scratch_shapes=[
            pltpu.VMEM((16, 1024), F32), pltpu.VMEM((16, 4096), F32), pltpu.VMEM((8, 128), jnp.int32), pltpu.VMEM((16, 1024), F32),
            pltpu.VMEM((1024, 128), BF16), pltpu.VMEM((128, 1024), BF16),
            pltpu.VMEM((1024, 1024), F32), pltpu.VMEM((1024, 1024), BF16), pltpu.VMEM((1024, 2048), F8),
            pltpu.VMEM((1024, 512), F32), pltpu.VMEM((1024, 512), BF16), pltpu.VMEM((512, 1024), BF16), pltpu.VMEM((1, 1024), F32),
            pltpu.VMEM((1024, 1024), BF16), pltpu.VMEM((1024, 2048), F8),
            pltpu.VMEM((1024, 1), F32), pltpu.VMEM((8, 128), F32),
            tile32(4, 2, 33), tile32(4, 33), tile32(4, 16, 2),
            tile(16, 3), tile(3, 16, 2), tile(15, 3), tile(3, 15, 2), tile(4, 3), tile(7, 3), tile(3, 7, 2), tile32(4, 2), tile(64, 4),
            dma((3,)), dma((4,)), dma, dma, dma, dma((4,)), dma((4,)), *[dma((4,))] * 8,
        ],
        compiler_params=pltpu.CompilerParams(collective_id=0, has_side_effects=True, vmem_limit_bytes=44 << 20),
    )(*[pltpu.with_memory_space_constraint(a, pltpu.HBM) for a in arrays])


def solution(mesh):
    both = ("group", "expert")
    return jax.shard_map(
        body,
        mesh=mesh,
        in_specs=(P(both, None, None), P(both, None, None), P(both, None, None), P(), P(), P(None, both), P(both)),
        out_specs=P(None, both),
        check_vma=False,
    )
```
